32 devices in a mesh: bead: 2 (over y), orb: 4 (over z), fit: 4 (over x, core).
Axes of the slice: x: 2, y: 2, z: 4, core: 2. Of those that a mesh axis runs over, the one named last changes fastest.
Arguments:
- half_ints: bfloat16 [8, 32, 128, 2432], P(('bead', 'orb'), 'fit'), parts along dimension 0, may hold values from -0.0625 to 0.0625
- orbital_coeffs: bfloat16 [8, 512, 128], P(('bead', 'orb')), parts along dimension 0, may hold values from -6 to 6
- block_owner: int32 [8], P('bead'), parts along dimension 0, may hold values from 0 to 3, as said below
- dom_start: int32 [8], P('bead'), parts along dimension 0, may hold values from 0 to 1407, as said below
- pair_list: int32 [20, 2], P('bead'), parts along dimension 0, may hold values from 0 to 3, as said below
Outputs:
- exch: float32 [8, 512, 128], P(('bead', 'orb'), 'fit'), parts along dimension 0
The draws below stay inside these ranges and needn't reach their ends.
There are 2 independent parts, one for each index of `bead`. The reference program is written for one: setup_inputs(seed, part) draws one part's arguments, and reference() takes and returns one part's arrays. A program takes and returns all parts, laid end to end along the dimension named above; each array names one. Nothing has to cross between parts.
Inputs may be any that keep to these rules, and one draw needn't show every extreme that they name: `block_owner`: A permutation; the block in slot s is held by the device of index s along orb. dom_start[b] - 448 * block_owner[b] lies in 0 to 63. `pair_list`: each row names two different blocks whose slots differ by at most 2; no row repeats; a block is the first block of at most 3 rows, and some block of exactly 3.
All inputs are finite; a program needn't handle non-finite values.
Results may differ from the reference program's by a relative error of at most 0.00053.
Values may be sent and summed in bfloat16 or wider, within the bound.
A program may use at most 64 MiB of HBM per device.

```python
import jax
import jax.numpy as jnp
from jax import lax

OCC = 128
DOM = 512
RANGE = 2
SPACING = 448
JIT = 64
HALF = 960
WIN = 2432
NBLK = 4
FIT = 32
NPAIR = 10


def layout(key):
    return jax.random.permutation(key, jnp.arange(NBLK, dtype=jnp.int32))


def draw_block_owner(key, part):
    placing = layout(key)
    return placing.astype(jnp.int32)


def draw_dom_start(key, part):
    placing = layout(key)
    key = jax.random.fold_in(key, 11)
    jitter = jax.random.randint(key, (NBLK,), 0, JIT, dtype=jnp.int32)
    jitter = jnp.where(placing == 0, 0, jnp.where(placing == NBLK - 1, JIT - 1, jitter))
    return (placing * SPACING + jitter).astype(jnp.int32)


def draw_pair_list(key, part):
    placing = layout(key)
    key = jax.random.fold_in(key, 23)
    key_pick, key_rank = jax.random.split(key)
    far_reach = min(RANGE, NBLK - 1)
    offsets = jnp.concatenate([jnp.arange(-far_reach, 0, dtype=jnp.int32), jnp.arange(1, far_reach + 1, dtype=jnp.int32)])
    slot_ids = jnp.arange(NBLK, dtype=jnp.int32)[:, None]
    target_slot = slot_ids + offsets[None, :]
    inside = (target_slot >= 0) & (target_slot < NBLK)
    if NBLK > 2 * far_reach:
        low_slot = far_reach
        slot_span = NBLK - 2 * far_reach
    else:
        low_slot = 0
        slot_span = 1
    chosen = low_slot + jax.random.randint(key_pick, (), 0, slot_span, dtype=jnp.int32)
    scores = jax.random.permutation(key_rank, jnp.arange(NBLK * 2 * far_reach, dtype=jnp.int32)).reshape(NBLK, 2 * far_reach)
    scores = scores + jnp.where(slot_ids == chosen, NBLK * 2 * far_reach, 0)
    scores = jnp.where(inside, scores, -1)
    _, chosen_idx = lax.top_k(scores.reshape(-1), NPAIR)
    source_slot = chosen_idx // (2 * far_reach)
    target_flat = target_slot.reshape(-1)[chosen_idx]
    block_at = jnp.argsort(placing, stable=True).astype(jnp.int32)
    return jnp.stack([block_at[source_slot], block_at[target_flat]], axis=1).astype(jnp.int32)


def shard_levels(stream_key, dims, shards, smallest, high):
    def one(position, shards_of):
        draws = jax.random.uniform(jax.random.fold_in(jax.random.fold_in(stream_key, 6), position), (shards_of,), jnp.float32, smallest / len(shards), high / len(shards))
        return jnp.repeat(jnp.exp(draws), dims[position] // shards_of).reshape((-1,) + (1,) * (len(dims) - position - 1))

    level = one(*shards[0])
    for cut in shards[1:]:
        level = level * one(*cut)
    return level


def gaussian(stream_key, shape, scale, bound, cuts=(), kind=jnp.bfloat16):
    entries = scale * jax.random.normal(stream_key, shape, jnp.float32)
    if cuts:
        entries = entries * shard_levels(stream_key, shape, cuts, -0.22, 0.18)
    return jnp.clip(entries, -bound, bound).astype(kind)


def setup_inputs(seed: int = 0, part: int = 0) -> dict:
    splits = jax.random.split(jax.random.key(seed), 6)
    own_keys = jax.random.split(jax.random.fold_in(splits[5], part), 6)
    half_ints = gaussian(own_keys[0], (NBLK, FIT, OCC, WIN), (DOM * 16) ** -0.5, 0.0625, ((0, 4), (1, 4)))
    orbital_coeffs = gaussian(own_keys[1], (NBLK, DOM, OCC), 1.0, 6.0, ((0, 4),))
    block_owner = draw_block_owner(jax.random.fold_in(jax.random.fold_in(splits[5], part), 71), part)
    dom_start = draw_dom_start(jax.random.fold_in(jax.random.fold_in(splits[5], part), 71), part)
    pair_list = draw_pair_list(jax.random.fold_in(jax.random.fold_in(splits[5], part), 71), part)
    return {"half_ints": half_ints, "orbital_coeffs": orbital_coeffs, "block_owner": block_owner, "dom_start": dom_start, "pair_list": pair_list}


def pair_term(window_all, coeff_block, offset):
    fit_count = window_all.shape[0]
    occ_count = window_all.shape[1]
    dom_count = coeff_block.shape[0]
    window = lax.dynamic_slice(window_all, (jnp.int32(0), jnp.int32(0), offset.astype(jnp.int32)), (fit_count, occ_count, dom_count))
    window = window.reshape(fit_count * occ_count, dom_count)
    fitted = jnp.dot(window, coeff_block, preferred_element_type=jnp.float32).astype(jnp.bfloat16)
    return lax.dot_general(window, fitted, (((0,), (0,)), ((), ())), preferred_element_type=jnp.float32)


def reference(half_ints, orbital_coeffs, block_owner, dom_start, pair_list):
    block_ids = jnp.arange(NBLK, dtype=jnp.int32)
    every_pair = jnp.concatenate([jnp.stack([block_ids, block_ids], axis=1), pair_list.astype(jnp.int32)], axis=0)

    def visit(accumulated, pair_row):
        first_block = pair_row[0]
        second_block = pair_row[1]
        slot_first = block_owner[first_block]
        slot_second = block_owner[second_block]
        offset = dom_start[second_block] - dom_start[first_block] + HALF
        term = pair_term(half_ints[slot_first], orbital_coeffs[slot_second], offset)
        return accumulated.at[slot_second].add(term), None

    start_acc = jnp.zeros((NBLK, DOM, OCC), jnp.float32)
    result, _ = lax.scan(visit, start_acc, every_pair)
    return result
```

```python
import functools

import jax
import jax.numpy as jnp
from jax import lax
from jax.experimental import pallas as pl
from jax.experimental.pallas import tpu as pltpu
from jax.sharding import PartitionSpec as P

MESH = pl.DeviceIdType.MESH
RANGE = 2
SPACING = 448
JIT = 64
LANE = 128
PAD = 192


def columns_of(shift, half, dom, win):
    low = (half + SPACING * shift - JIT + 1) // LANE * LANE
    high = -(-(half + SPACING * shift + JIT - 1 + dom) // LANE) * LANE
    if shift == 0:
        low, high = half // LANE * LANE, -(-(half + dom) // LANE) * LANE
    return max(low, 0), min(high, win)


def kernel(
    sizes, owner_ref, start_ref, pair_ref, ints_hbm, coeff_hbm, out_ref,
    ints, coeff, got, padded, wide, away, keep, got1, sum1, got2, sum2, got3,
    ints_sem, coeff_sem, csend, crecv, fsend, frecv, send1, recv1, send2, recv2, send3, recv3,
):
    orb_count, fit_count, reach = sizes
    shifts = [s for s in range(-reach, reach + 1) if s != 0]
    order = [0] + [sign * k for k in range(1, reach + 1) for sign in (-1, 1)]
    slot = {s: s + reach for s in range(-reach, reach + 1)}
    rows, win = ints.shape
    dom = 2 * coeff.shape[1]
    half = (win - dom) // 2
    quarter = out_ref.shape[0]
    me = lax.axis_index("orb")
    fit = lax.axis_index("fit")
    low = lax.rem(fit, 2)
    high = fit // 2
    pal1 = {"fit": high * 2 + 1 - low}
    pal2 = {"fit": (1 - high) * 2 + low}

    def inside(s):
        return (me + s >= 0) & (me + s < orb_count)

    def remote(src, dst, send, recv, device):
        return pltpu.make_async_remote_copy(
            src_ref=src, dst_ref=dst, send_sem=send, recv_sem=recv,
            device_id=device, device_id_type=MESH,
        )

    coeff_copy = pltpu.make_async_copy(coeff_hbm, coeff, coeff_sem)
    coeff_copy.start()
    spans = {s: columns_of(s, half, dom, win) for s in order}
    cuts = [spans[0]]
    for k in range(1, reach + 1):
        cuts = cuts + [(spans[-k][0], min(c[0] for c in cuts)), (max(c[1] for c in cuts), spans[k][1])]
    copies = []
    for n, (a, b) in enumerate(cuts):
        copy = pltpu.make_async_copy(ints_hbm.at[:, a:b], ints.at[:, a:b], ints_sem.at[n])
        copy.start()
        copies.append(copy)

    barrier = pltpu.get_barrier_semaphore()
    for pal in (pal1, pal2):
        pl.semaphore_signal(barrier, inc=1, device_id=pal, device_id_type=MESH)
    expected = jnp.int32(2)
    for s in shifts:
        @pl.when(inside(s))
        def _(s=s):
            pl.semaphore_signal(barrier, inc=1, device_id={"orb": me + s}, device_id_type=MESH)
        expected = expected + inside(s).astype(jnp.int32)

    zeros = jnp.zeros((PAD, padded.shape[1]), jnp.float32)
    padded[0:PAD] = zeros
    padded[PAD + dom : 2 * PAD + dom] = zeros

    blocks = owner_ref.shape[0]
    pairs = pair_ref.shape[0]
    wanted = list(range(-reach, reach + 1))

    def find(b, found):
        held = owner_ref[b]
        begin = start_ref[b]
        new = []
        for n, s in enumerate(wanted):
            hit = held == me + s
            new.append((jnp.where(hit, b, found[n][0]), jnp.where(hit, begin, found[n][1])))
        return tuple(new)

    found = tuple((jnp.int32(-1), jnp.int32(0)) for _ in wanted)
    found = lax.fori_loop(0, blocks, find, found, unroll=blocks <= 8)
    my_block, my_start = found[reach]

    def scan(p, listed):
        first = pair_ref[p, 0] == my_block
        second = pair_ref[p, 1]
        return tuple(
            jnp.where(first & (second == found[slot[s]][0]), 1, listed[n]) for n, s in enumerate(shifts)
        )

    listed = lax.fori_loop(0, pairs, scan, tuple(jnp.int32(0) for _ in shifts), unroll=pairs <= 16)
    listed = dict(zip(shifts, listed))

    pl.semaphore_wait(barrier, expected)

    coeff_out = {}
    for s in [k for k in order if k != 0]:
        coeff_out[s] = remote(
            coeff_hbm.at[low], got.at[slot[-s], low], csend.at[slot[s]], crecv.at[slot[-s]], {"orb": me + s}
        )

        @pl.when(inside(s))
        def _(s=s):
            coeff_out[s].start()

    def arrival(s):
        return remote(
            coeff_hbm.at[low], got.at[slot[s], low], csend.at[slot[-s]], crecv.at[slot[s]], {"orb": me + s}
        )

    def forward(s):
        return remote(got.at[slot[s], low], got.at[slot[s], low], fsend.at[slot[s]], frecv.at[slot[s]], pal1)

    def other_half(s):
        return remote(got.at[slot[s], low], got.at[slot[s], 1 - low], fsend.at[slot[s]], frecv.at[slot[s]], pal1)

    def stage1(s):
        n = slot[s]
        return remote(away.at[n], got1.at[n], send1.at[n], recv1.at[n], pal1)

    def stage2(s):
        n = slot[s]
        return remote(sum1.at[n, 1 - high], got2.at[n], send2.at[n], recv2.at[n], pal2)

    def stage3(s):
        return remote(sum2.at[slot[s]], got3.at[slot[-s]], send3.at[slot[s]], recv3.at[slot[-s]], {"orb": me + s})

    def compute(s):
        a, b = spans[s]
        width = b - a
        if s == 0:
            block = coeff[...]
            offset = jnp.int32(half - a)
        else:
            block = got[slot[s]]
            offset = jnp.clip(
                found[slot[s]][1] - my_start + half - a, max(0, width - dom - PAD), min(PAD, width - dom)
            )
        padded[PAD : PAD + dom] = block.reshape(dom, block.shape[-1]).astype(jnp.float32)
        shifted = padded[pl.ds(PAD - offset, width), :].astype(jnp.bfloat16)
        window = ints[:, a:b]
        fitted = jnp.dot(window, shifted, preferred_element_type=jnp.float32).astype(jnp.bfloat16)
        wide[0:width] = lax.dot_general(
            window, fitted, (((0,), (0,)), ((), ())), preferred_element_type=jnp.float32
        )
        for x in range(2):
            away[slot[s], x] = wide[pl.ds(offset + (2 * x + 1 - low) * quarter, quarter), :]
            keep[slot[s], x] = wide[pl.ds(offset + (2 * x + low) * quarter, quarter), :]

    def when(s, do):
        if s == 0:
            do()
        else:
            pl.when(inside(s))(do)

    def pass_on(s):
        def do():
            arrival(s).wait_recv()
            forward(s).start()
        when(s, do)

    def work(s):
        def do():
            if s != 0:
                other_half(s).wait_recv()
            compute(s)
            stage1(s).start()
        when(s, do)

    def first(s):
        def do():
            stage1(s).wait_recv()
            sum1[slot[s]] = keep[slot[s]] + got1[slot[s]]
            stage2(s).start()
        when(s, do)

    def second(s):
        def do():
            stage2(s).wait_recv()
            total = sum1[slot[s], high] + got2[slot[s]]
            if s == 0:
                sum2[slot[s]] = total
            else:
                sum2[slot[s]] = jnp.where(listed[s] > 0, total, 0.0)
                stage3(s).start()
        when(s, do)

    coeff_copy.wait()
    copies[0].wait()
    work(0)
    pass_on(-1)
    pass_on(1)
    first(0)
    waiting = []
    previous = 0
    for n, s in enumerate(order[1:]):
        copies[n + 1].wait()
        work(s)
        if s < 0 and abs(s) < reach:
            pass_on(s - 1)
            pass_on(1 - s)
        if previous != 0:
            first(previous)
        waiting.append(previous)
        if n >= 1:
            second(waiting[n - 1])
        previous = s
    first(previous)
    waiting.append(previous)
    for s in waiting[len(order) - 2 :]:
        second(s)

    total = sum2[slot[0]]
    out_ref[...] = total
    for s in shifts:
        def take(s=s):
            stage3(-s).wait_recv()
            out_ref[...] += got3[slot[s]]
        when(s, take)

    for s in order:
        def drain(s=s):
            stage1(s).wait_send()
            stage2(s).wait_send()
            if s != 0:
                coeff_out[s].wait_send()
                forward(s).wait_send()
                stage3(s).wait_send()
        when(s, drain)


def local(sizes, half_ints, orbital_coeffs, block_owner, dom_start, pair_list):
    orb_count, fit_count, reach = sizes
    _, fits, occ, win = half_ints.shape
    dom = orbital_coeffs.shape[1]
    ints = half_ints.reshape(fits * occ, win)
    coeffs = orbital_coeffs.reshape(2, dom // 2, occ)
    quarter = dom // fit_count
    slots = 2 * reach + 1
    f32 = jnp.float32
    dma = pltpu.SemaphoreType.DMA
    out = pl.pallas_call(
        functools.partial(kernel, sizes),
        out_shape=jax.ShapeDtypeStruct((quarter, occ), f32),
        in_specs=[pl.BlockSpec(memory_space=pltpu.SMEM)] * 3 + [pl.BlockSpec(memory_space=pl.ANY)] * 2,
        out_specs=pl.BlockSpec(memory_space=pltpu.VMEM),
        scratch_shapes=[
            pltpu.VMEM((fits * occ, win), jnp.bfloat16),
            pltpu.VMEM((2, dom // 2, occ), jnp.bfloat16),
            pltpu.VMEM((slots, 2, dom // 2, occ), jnp.bfloat16),
            pltpu.VMEM((2 * PAD + dom, occ), f32),
            pltpu.VMEM((dom + 256, occ), f32),
            pltpu.VMEM((slots, 2, quarter, occ), f32),
            pltpu.VMEM((slots, 2, quarter, occ), f32),
            pltpu.VMEM((slots, 2, quarter, occ), f32),
            pltpu.VMEM((slots, 2, quarter, occ), f32),
            pltpu.VMEM((slots, quarter, occ), f32),
            pltpu.VMEM((slots, quarter, occ), f32),
            pltpu.VMEM((slots, quarter, occ), f32),
            dma((slots,)),
            dma,
        ] + [dma((slots,))] * 10,
        compiler_params=pltpu.CompilerParams(
            collective_id=0, has_side_effects=True, vmem_limit_bytes=48 * 1024 * 1024
        ),
    )(block_owner, dom_start, pair_list, ints, coeffs)
    return out[None]


def solution(mesh):
    orb_count = mesh.shape["orb"]
    sizes = (orb_count, mesh.shape["fit"], min(RANGE, orb_count - 1))
    return jax.shard_map(
        functools.partial(local, sizes),
        mesh=mesh,
        in_specs=(
            P(("bead", "orb"), "fit", None, None),
            P(("bead", "orb"), None, None),
            P("bead"),
            P("bead"),
            P("bead", None),
        ),
        out_specs=P(("bead", "orb"), "fit", None),
        check_vma=False,
    )
```

```python
import functools

import jax
import jax.numpy as jnp
from jax import lax
from jax.experimental import pallas as pl
from jax.experimental.pallas import tpu as pltpu
from jax.sharding import PartitionSpec as P

MESH = pl.DeviceIdType.MESH
RANGE = 2
SPACING = 448
JIT = 64
LANE = 128
PAD = 192


def columns_of(shift, half, dom, win):
    low = (half + SPACING * shift - JIT + 1) // LANE * LANE
    high = -(-(half + SPACING * shift + JIT - 1 + dom) // LANE) * LANE
    if shift == 0:
        low, high = half // LANE * LANE, -(-(half + dom) // LANE) * LANE
    return max(low, 0), min(high, win)


def kernel(
    sizes, owner_hbm, start_hbm, pair_hbm, ints_hbm, coeff_hbm, out_ref,
    owner_ref, start_ref, pair_ref, table_sem,
    ints, coeff, got, padded, wide, away, keep, got1, sum1, got2, sum2, got3,
    ints_sem, coeff_sem, csend, crecv, fsend, frecv, send1, recv1, send2, recv2, send3, recv3,
):
    orb_count, fit_count, reach = sizes
    shifts = [s for s in range(-reach, reach + 1) if s != 0]
    order = [0] + [sign * k for k in range(1, reach + 1) for sign in (-1, 1)]
    slot = {s: s + reach for s in range(-reach, reach + 1)}
    rows, win = ints.shape
    dom = 2 * coeff.shape[1]
    half = (win - dom) // 2
    quarter = out_ref.shape[0]
    me = lax.axis_index("orb")
    fit = lax.axis_index("fit")
    low = lax.rem(fit, 2)
    high = fit // 2
    pal1 = {"fit": high * 2 + 1 - low}
    pal2 = {"fit": (1 - high) * 2 + low}

    def inside(s):
        return (me + s >= 0) & (me + s < orb_count)

    def remote(src, dst, send, recv, device):
        return pltpu.make_async_remote_copy(
            src_ref=src, dst_ref=dst, send_sem=send, recv_sem=recv,
            device_id=device, device_id_type=MESH,
        )

    tables = [
        pltpu.make_async_copy(src, dst, table_sem.at[n])
        for n, (src, dst) in enumerate(
            ((owner_hbm, owner_ref), (start_hbm, start_ref), (pair_hbm, pair_ref))
        )
    ]
    for table in tables:
        table.start()
    coeff_copy = pltpu.make_async_copy(coeff_hbm, coeff, coeff_sem)
    coeff_copy.start()
    spans = {s: columns_of(s, half, dom, win) for s in order}
    cuts = [spans[0]]
    for k in range(1, reach + 1):
        cuts = cuts + [(spans[-k][0], min(c[0] for c in cuts)), (max(c[1] for c in cuts), spans[k][1])]
    copies = []
    for n, (a, b) in enumerate(cuts):
        copy = pltpu.make_async_copy(ints_hbm.at[:, a:b], ints.at[:, a:b], ints_sem.at[n])
        copy.start()
        copies.append(copy)

    barrier = pltpu.get_barrier_semaphore()
    for pal in (pal1, pal2):
        pl.semaphore_signal(barrier, inc=1, device_id=pal, device_id_type=MESH)
    expected = jnp.int32(2)
    for s in shifts:
        @pl.when(inside(s))
        def _(s=s):
            pl.semaphore_signal(barrier, inc=1, device_id={"orb": me + s}, device_id_type=MESH)
        expected = expected + inside(s).astype(jnp.int32)

    zeros = jnp.zeros((PAD, padded.shape[1]), jnp.float32)
    padded[0:PAD] = zeros
    padded[PAD + dom : 2 * PAD + dom] = zeros

    for table in tables:
        table.wait()
    blocks = owner_ref.shape[0]
    pairs = pair_ref.shape[1]
    wanted = list(range(-reach, reach + 1))

    def find(b, found):
        held = owner_ref[b]
        begin = start_ref[b]
        new = []
        for n, s in enumerate(wanted):
            hit = held == me + s
            new.append((jnp.where(hit, b, found[n][0]), jnp.where(hit, begin, found[n][1])))
        return tuple(new)

    found = tuple((jnp.int32(-1), jnp.int32(0)) for _ in wanted)
    found = lax.fori_loop(0, blocks, find, found, unroll=blocks <= 8)
    my_block, my_start = found[reach]

    def scan(p, listed):
        first = pair_ref[0, p] == my_block
        second = pair_ref[1, p]
        return tuple(
            jnp.where(first & (second == found[slot[s]][0]), 1, listed[n]) for n, s in enumerate(shifts)
        )

    listed = lax.fori_loop(0, pairs, scan, tuple(jnp.int32(0) for _ in shifts), unroll=pairs <= 16)
    listed = dict(zip(shifts, listed))

    pl.semaphore_wait(barrier, expected)

    coeff_out = {}
    for s in [k for k in order if k != 0]:
        coeff_out[s] = remote(
            coeff_hbm.at[low], got.at[slot[-s], low], csend.at[slot[s]], crecv.at[slot[-s]], {"orb": me + s}
        )

        @pl.when(inside(s))
        def _(s=s):
            coeff_out[s].start()

    def arrival(s):
        return remote(
            coeff_hbm.at[low], got.at[slot[s], low], csend.at[slot[-s]], crecv.at[slot[s]], {"orb": me + s}
        )

    def forward(s):
        return remote(got.at[slot[s], low], got.at[slot[s], low], fsend.at[slot[s]], frecv.at[slot[s]], pal1)

    def other_half(s):
        return remote(got.at[slot[s], low], got.at[slot[s], 1 - low], fsend.at[slot[s]], frecv.at[slot[s]], pal1)

    def stage1(s):
        n = slot[s]
        return remote(away.at[n], got1.at[n], send1.at[n], recv1.at[n], pal1)

    def stage2(s):
        n = slot[s]
        return remote(sum1.at[n, 1 - high], got2.at[n], send2.at[n], recv2.at[n], pal2)

    def stage3(s):
        return remote(sum2.at[slot[s]], got3.at[slot[-s]], send3.at[slot[s]], recv3.at[slot[-s]], {"orb": me + s})

    def compute(s):
        a, b = spans[s]
        width = b - a
        if s == 0:
            block = coeff[...]
            offset = jnp.int32(half - a)
        else:
            block = got[slot[s]]
            offset = jnp.clip(
                found[slot[s]][1] - my_start + half - a, max(0, width - dom - PAD), min(PAD, width - dom)
            )
        padded[PAD : PAD + dom] = block.reshape(dom, block.shape[-1]).astype(jnp.float32)
        shifted = padded[pl.ds(PAD - offset, width), :].astype(jnp.bfloat16)
        window = ints[:, a:b]
        fitted = jnp.dot(window, shifted, preferred_element_type=jnp.float32).astype(jnp.bfloat16)
        wide[0:width] = lax.dot_general(
            window, fitted, (((0,), (0,)), ((), ())), preferred_element_type=jnp.float32
        )
        for x in range(2):
            away[slot[s], x] = wide[pl.ds(offset + (2 * x + 1 - low) * quarter, quarter), :]
            keep[slot[s], x] = wide[pl.ds(offset + (2 * x + low) * quarter, quarter), :]

    def when(s, do):
        if s == 0:
            do()
        else:
            pl.when(inside(s))(do)

    def pass_on(s):
        def do():
            arrival(s).wait_recv()
            forward(s).start()
        when(s, do)

    def work(s):
        def do():
            if s != 0:
                other_half(s).wait_recv()
            compute(s)
            stage1(s).start()
        when(s, do)

    def first(s):
        def do():
            stage1(s).wait_recv()
            sum1[slot[s]] = keep[slot[s]] + got1[slot[s]]
            stage2(s).start()
        when(s, do)

    def second(s):
        def do():
            stage2(s).wait_recv()
            total = sum1[slot[s], high] + got2[slot[s]]
            if s == 0:
                sum2[slot[s]] = total
            else:
                sum2[slot[s]] = jnp.where(listed[s] > 0, total, 0.0)
                stage3(s).start()
        when(s, do)

    coeff_copy.wait()
    copies[0].wait()
    work(0)
    pass_on(-1)
    pass_on(1)
    first(0)
    waiting = []
    previous = 0
    for n, s in enumerate(order[1:]):
        copies[n + 1].wait()
        work(s)
        if s < 0 and abs(s) < reach:
            pass_on(s - 1)
            pass_on(1 - s)
        if previous != 0:
            first(previous)
        waiting.append(previous)
        if n >= 1:
            second(waiting[n - 1])
        previous = s
    first(previous)
    waiting.append(previous)
    for s in waiting[len(order) - 2 :]:
        second(s)

    total = sum2[slot[0]]
    out_ref[...] = total
    for s in shifts:
        def take(s=s):
            stage3(-s).wait_recv()
            out_ref[...] += got3[slot[s]]
        when(s, take)

    for s in order:
        def drain(s=s):
            stage1(s).wait_send()
            stage2(s).wait_send()
            if s != 0:
                coeff_out[s].wait_send()
                forward(s).wait_send()
                stage3(s).wait_send()
        when(s, drain)


def local(sizes, half_ints, orbital_coeffs, block_owner, dom_start, pair_list):
    orb_count, fit_count, reach = sizes
    _, fits, occ, win = half_ints.shape
    dom = orbital_coeffs.shape[1]
    ints = half_ints.reshape(fits * occ, win)
    coeffs = orbital_coeffs.reshape(2, dom // 2, occ)
    quarter = dom // fit_count
    slots = 2 * reach + 1
    f32 = jnp.float32
    dma = pltpu.SemaphoreType.DMA
    out = pl.pallas_call(
        functools.partial(kernel, sizes),
        out_shape=jax.ShapeDtypeStruct((quarter, occ), f32),
        in_specs=[pl.BlockSpec(memory_space=pltpu.HBM)] * 5,
        out_specs=pl.BlockSpec(memory_space=pltpu.VMEM),
        scratch_shapes=[
            pltpu.SMEM(block_owner.shape, jnp.int32),
            pltpu.SMEM(dom_start.shape, jnp.int32),
            pltpu.SMEM(pair_list.shape[::-1], jnp.int32),
            dma((3,)),
            pltpu.VMEM((fits * occ, win), jnp.bfloat16),
            pltpu.VMEM((2, dom // 2, occ), jnp.bfloat16),
            pltpu.VMEM((slots, 2, dom // 2, occ), jnp.bfloat16),
            pltpu.VMEM((2 * PAD + dom, occ), f32),
            pltpu.VMEM((dom + 256, occ), f32),
            pltpu.VMEM((slots, 2, quarter, occ), f32),
            pltpu.VMEM((slots, 2, quarter, occ), f32),
            pltpu.VMEM((slots, 2, quarter, occ), f32),
            pltpu.VMEM((slots, 2, quarter, occ), f32),
            pltpu.VMEM((slots, quarter, occ), f32),
            pltpu.VMEM((slots, quarter, occ), f32),
            pltpu.VMEM((slots, quarter, occ), f32),
            dma((slots,)),
            dma,
        ] + [dma((slots,))] * 10,
        compiler_params=pltpu.CompilerParams(
            collective_id=0, has_side_effects=True, vmem_limit_bytes=64 * 1024 * 1024
        ),
    )(block_owner, dom_start, pair_list.T, ints, coeffs)
    return out[None]


def solution(mesh):
    orb_count = mesh.shape["orb"]
    sizes = (orb_count, mesh.shape["fit"], min(RANGE, orb_count - 1))
    return jax.shard_map(
        functools.partial(local, sizes),
        mesh=mesh,
        in_specs=(
            P(("bead", "orb"), "fit", None, None),
            P(("bead", "orb"), None, None),
            P("bead"),
            P("bead"),
            P("bead", None),
        ),
        out_specs=P(("bead", "orb"), "fit", None),
        check_vma=False,
    )
```

```python
import functools

import jax
import jax.numpy as jnp
from jax import lax
from jax.experimental import pallas as pl
from jax.experimental.pallas import tpu as pltpu
from jax.sharding import PartitionSpec as P

MESH = pl.DeviceIdType.MESH
RANGE = 2
SPACING = 448
JIT = 64
LANE = 128
PAD = 192


def columns_of(shift, half, dom, win):
    low = (half + SPACING * shift - JIT + 1) // LANE * LANE
    high = -(-(half + SPACING * shift + JIT - 1 + dom) // LANE) * LANE
    if shift == 0:
        low, high = half // LANE * LANE, -(-(half + dom) // LANE) * LANE
    return max(low, 0), min(high, win)


def kernel(
    sizes, owner_hbm, start_hbm, pair_hbm, ints_hbm, coeff_hbm, out_ref,
    owner_ref, start_ref, pair_ref, table_sem,
    ints, coeff, got, padded, wide, away, keep, got1, sum1, got2, sum2, got3,
    ints_sem, coeff_sem, csend, crecv, fsend, frecv, send1, recv1, send2, recv2, send3, recv3,
):
    orb_count, fit_count, reach = sizes
    shifts = [s for s in range(-reach, reach + 1) if s != 0]
    order = [0] + [sign * k for k in range(reach, 0, -1) for sign in (-1, 1)]
    slot = {s: s + reach for s in range(-reach, reach + 1)}
    rows, win = ints.shape
    dom = 2 * coeff.shape[1]
    half = (win - dom) // 2
    quarter = out_ref.shape[0]
    me = lax.axis_index("orb")
    fit = lax.axis_index("fit")
    low = lax.rem(fit, 2)
    high = fit // 2
    pal1 = {"fit": high * 2 + 1 - low}
    pal2 = {"fit": (1 - high) * 2 + low}

    def inside(s):
        return (me + s >= 0) & (me + s < orb_count)

    def remote(src, dst, send, recv, device):
        return pltpu.make_async_remote_copy(
            src_ref=src, dst_ref=dst, send_sem=send, recv_sem=recv,
            device_id=device, device_id_type=MESH,
        )

    tables = [
        pltpu.make_async_copy(src, dst, table_sem.at[n])
        for n, (src, dst) in enumerate(
            ((owner_hbm, owner_ref), (start_hbm, start_ref), (pair_hbm, pair_ref))
        )
    ]
    for table in tables:
        table.start()
    coeff_copy = pltpu.make_async_copy(coeff_hbm, coeff, coeff_sem)
    coeff_copy.start()
    spans = {s: columns_of(s, half, dom, win) for s in order}
    cuts = [spans[0]]
    for k in range(1, reach + 1):
        cuts = cuts + [(spans[-k][0], min(c[0] for c in cuts)), (max(c[1] for c in cuts), spans[k][1])]
    copies = []
    for n, (a, b) in enumerate(cuts):
        copy = pltpu.make_async_copy(ints_hbm.at[:, a:b], ints.at[:, a:b], ints_sem.at[n])
        copy.start()
        copies.append(copy)

    barrier = pltpu.get_barrier_semaphore()
    for pal in (pal1, pal2):
        pl.semaphore_signal(barrier, inc=1, device_id=pal, device_id_type=MESH)
    expected = jnp.int32(2)
    for s in shifts:
        @pl.when(inside(s))
        def _(s=s):
            pl.semaphore_signal(barrier, inc=1, device_id={"orb": me + s}, device_id_type=MESH)
        expected = expected + inside(s).astype(jnp.int32)

    zeros = jnp.zeros((PAD, padded.shape[1]), jnp.float32)
    padded[0:PAD] = zeros
    padded[PAD + dom : 2 * PAD + dom] = zeros

    for table in tables:
        table.wait()
    blocks = owner_ref.shape[0]
    pairs = pair_ref.shape[1]
    wanted = list(range(-reach, reach + 1))

    def find(b, found):
        held = owner_ref[b]
        begin = start_ref[b]
        new = []
        for n, s in enumerate(wanted):
            hit = held == me + s
            new.append((jnp.where(hit, b, found[n][0]), jnp.where(hit, begin, found[n][1])))
        return tuple(new)

    found = tuple((jnp.int32(-1), jnp.int32(0)) for _ in wanted)
    found = lax.fori_loop(0, blocks, find, found, unroll=blocks <= 8)
    my_block, my_start = found[reach]

    def scan(p, listed):
        first = pair_ref[0, p] == my_block
        second = pair_ref[1, p]
        return tuple(
            jnp.where(first & (second == found[slot[s]][0]), 1, listed[n]) for n, s in enumerate(shifts)
        )

    listed = lax.fori_loop(0, pairs, scan, tuple(jnp.int32(0) for _ in shifts), unroll=pairs <= 16)
    listed = dict(zip(shifts, listed))

    pl.semaphore_wait(barrier, expected)

    coeff_out = {}
    for s in [k for k in order if k != 0]:
        coeff_out[s] = remote(
            coeff_hbm.at[low], got.at[slot[-s], low], csend.at[slot[s]], crecv.at[slot[-s]], {"orb": me + s}
        )

        @pl.when(inside(s))
        def _(s=s):
            coeff_out[s].start()

    def arrival(s):
        return remote(
            coeff_hbm.at[low], got.at[slot[s], low], csend.at[slot[-s]], crecv.at[slot[s]], {"orb": me + s}
        )

    def forward(s):
        return remote(got.at[slot[s], low], got.at[slot[s], low], fsend.at[slot[s]], frecv.at[slot[s]], pal1)

    def other_half(s):
        return remote(got.at[slot[s], low], got.at[slot[s], 1 - low], fsend.at[slot[s]], frecv.at[slot[s]], pal1)

    def stage1(s):
        n = slot[s]
        return remote(away.at[n], got1.at[n], send1.at[n], recv1.at[n], pal1)

    def stage2(s):
        n = slot[s]
        return remote(sum1.at[n, 1 - high], got2.at[n], send2.at[n], recv2.at[n], pal2)

    def stage3(s):
        return remote(sum2.at[slot[s]], got3.at[slot[-s]], send3.at[slot[s]], recv3.at[slot[-s]], {"orb": me + s})

    def compute(s):
        a, b = spans[s]
        width = b - a
        if s == 0:
            block = coeff[...]
            offset = jnp.int32(half - a)
        else:
            block = got[slot[s]]
            offset = jnp.clip(
                found[slot[s]][1] - my_start + half - a, max(0, width - dom - PAD), min(PAD, width - dom)
            )
        padded[PAD : PAD + dom] = block.reshape(dom, block.shape[-1]).astype(jnp.float32)
        shifted = padded[pl.ds(PAD - offset, width), :].astype(jnp.bfloat16)
        window = ints[:, a:b]
        fitted = lax.dot_general(
            shifted, window, (((0,), (1,)), ((), ())), preferred_element_type=jnp.float32
        ).astype(jnp.bfloat16)
        wide[0:width] = jnp.dot(fitted, window, preferred_element_type=jnp.float32).T
        for x in range(2):
            away[slot[s], x] = wide[pl.ds(offset + (2 * x + 1 - low) * quarter, quarter), :]
            keep[slot[s], x] = wide[pl.ds(offset + (2 * x + low) * quarter, quarter), :]

    def when(s, do):
        if s == 0:
            do()
        else:
            pl.when(inside(s))(do)

    def pass_on(s):
        def do():
            arrival(s).wait_recv()
            forward(s).start()
        when(s, do)

    def work(s):
        def do():
            if s != 0:
                other_half(s).wait_recv()
            compute(s)
            stage1(s).start()
        when(s, do)

    def first(s):
        def do():
            stage1(s).wait_recv()
            sum1[slot[s]] = keep[slot[s]] + got1[slot[s]]
            stage2(s).start()
        when(s, do)

    def second(s):
        def do():
            stage2(s).wait_recv()
            total = sum1[slot[s], high] + got2[slot[s]]
            if s == 0:
                sum2[slot[s]] = total
            else:
                sum2[slot[s]] = jnp.where(listed[s] > 0, total, 0.0)
                stage3(s).start()
        when(s, do)

    coeff_copy.wait()
    copies[0].wait()
    work(0)
    for s in order[1:3]:
        pass_on(s)
    first(0)
    for copy in copies[1:]:
        copy.wait()
    for n, s in enumerate(order[1:]):
        work(s)
        if n + 3 < len(order):
            pass_on(order[n + 3])
        if n > 0:
            first(order[n])
    second(order[1])
    second(order[2])
    first(order[-1])
    for s in order[3:] + [0]:
        second(s)

    total = sum2[slot[0]]
    out_ref[...] = total
    for s in shifts:
        def take(s=s):
            stage3(-s).wait_recv()
            out_ref[...] += got3[slot[s]]
        when(s, take)

    for s in order:
        def drain(s=s):
            stage1(s).wait_send()
            stage2(s).wait_send()
            if s != 0:
                coeff_out[s].wait_send()
                forward(s).wait_send()
                stage3(s).wait_send()
        when(s, drain)


def local(sizes, half_ints, orbital_coeffs, block_owner, dom_start, pair_list):
    orb_count, fit_count, reach = sizes
    _, fits, occ, win = half_ints.shape
    dom = orbital_coeffs.shape[1]
    ints = half_ints.reshape(fits * occ, win)
    coeffs = orbital_coeffs.reshape(2, dom // 2, occ)
    quarter = dom // fit_count
    slots = 2 * reach + 1
    f32 = jnp.float32
    dma = pltpu.SemaphoreType.DMA
    out = pl.pallas_call(
        functools.partial(kernel, sizes),
        out_shape=jax.ShapeDtypeStruct((quarter, occ), f32),
        in_specs=[pl.BlockSpec(memory_space=pltpu.HBM)] * 5,
        out_specs=pl.BlockSpec(memory_space=pltpu.VMEM),
        scratch_shapes=[
            pltpu.SMEM(block_owner.shape, jnp.int32),
            pltpu.SMEM(dom_start.shape, jnp.int32),
            pltpu.SMEM(pair_list.shape[::-1], jnp.int32),
            dma((3,)),
            pltpu.VMEM((fits * occ, win), jnp.bfloat16),
            pltpu.VMEM((2, dom // 2, occ), jnp.bfloat16),
            pltpu.VMEM((slots, 2, dom // 2, occ), jnp.bfloat16),
            pltpu.VMEM((2 * PAD + dom, occ), f32),
            pltpu.VMEM((dom + 256, occ), f32),
            pltpu.VMEM((slots, 2, quarter, occ), f32),
            pltpu.VMEM((slots, 2, quarter, occ), f32),
            pltpu.VMEM((slots, 2, quarter, occ), f32),
            pltpu.VMEM((slots, 2, quarter, occ), f32),
            pltpu.VMEM((slots, quarter, occ), f32),
            pltpu.VMEM((slots, quarter, occ), f32),
            pltpu.VMEM((slots, quarter, occ), f32),
            dma((slots,)),
            dma,
        ] + [dma((slots,))] * 10,
        compiler_params=pltpu.CompilerParams(
            collective_id=0, has_side_effects=True, vmem_limit_bytes=64 * 1024 * 1024
        ),
    )(block_owner, dom_start, pair_list.T, ints, coeffs)
    return out[None]


def solution(mesh):
    orb_count = mesh.shape["orb"]
    sizes = (orb_count, mesh.shape["fit"], min(RANGE, orb_count - 1))
    return jax.shard_map(
        functools.partial(local, sizes),
        mesh=mesh,
        in_specs=(
            P(("bead", "orb"), "fit", None, None),
            P(("bead", "orb"), None, None),
            P("bead"),
            P("bead"),
            P("bead", None),
        ),
        out_specs=P(("bead", "orb"), "fit", None),
        check_vma=False,
    )
```

```python
import functools

import jax
import jax.numpy as jnp
from jax import lax
from jax.experimental import pallas as pl
from jax.experimental.pallas import tpu as pltpu
from jax.sharding import PartitionSpec as P

MESH = pl.DeviceIdType.MESH
STEPS = 16384.0
TAIL = 16
RANGE = 2
SPACING = 448
JIT = 64
LANE = 128
PAD = 192


def columns_of(shift, half, dom, win):
    low = (half + SPACING * shift - JIT + 1) // LANE * LANE
    high = -(-(half + SPACING * shift + JIT - 1 + dom) // LANE) * LANE
    if shift == 0:
        low, high = half // LANE * LANE, -(-(half + dom) // LANE) * LANE
    return max(low, 0), min(high, win)


def kernel(
    sizes, owner_hbm, start_hbm, pair_hbm, ints_hbm, coeff_hbm, out_ref,
    owner_ref, start_ref, pair_ref, table_sem,
    ints, coeff, got, padded, wide, away, keep, got1, sum1, got2, coded, got3,
    ints_sem, coeff_sem, csend, crecv, fsend, frecv, send1, recv1, send2, recv2, send3, recv3,
):
    orb_count, fit_count, reach = sizes
    shifts = [s for s in range(-reach, reach + 1) if s != 0]
    order = [0] + [sign * k for k in range(reach, 0, -1) for sign in (-1, 1)]
    slot = {s: s + reach for s in range(-reach, reach + 1)}
    rows, win = ints.shape
    dom = 2 * coeff.shape[1]
    half = (win - dom) // 2
    quarter = out_ref.shape[0]
    me = lax.axis_index("orb")
    fit = lax.axis_index("fit")
    low = lax.rem(fit, 2)
    high = fit // 2
    pal1 = {"fit": high * 2 + 1 - low}
    pal2 = {"fit": (1 - high) * 2 + low}

    def inside(s):
        return (me + s >= 0) & (me + s < orb_count)

    def remote(src, dst, send, recv, device):
        return pltpu.make_async_remote_copy(
            src_ref=src, dst_ref=dst, send_sem=send, recv_sem=recv,
            device_id=device, device_id_type=MESH,
        )

    tables = [
        pltpu.make_async_copy(src, dst, table_sem.at[n])
        for n, (src, dst) in enumerate(
            ((owner_hbm, owner_ref), (start_hbm, start_ref), (pair_hbm, pair_ref))
        )
    ]
    for table in tables:
        table.start()
    coeff_copy = pltpu.make_async_copy(coeff_hbm, coeff, coeff_sem)
    coeff_copy.start()
    spans = {s: columns_of(s, half, dom, win) for s in order}
    cuts = [spans[0]]
    for k in range(1, reach + 1):
        cuts = cuts + [(spans[-k][0], min(c[0] for c in cuts)), (max(c[1] for c in cuts), spans[k][1])]
    copies = []
    for n, (a, b) in enumerate(cuts):
        copy = pltpu.make_async_copy(ints_hbm.at[:, a:b], ints.at[:, a:b], ints_sem.at[n])
        copy.start()
        copies.append(copy)

    barrier = pltpu.get_barrier_semaphore()
    for pal in (pal1, pal2):
        pl.semaphore_signal(barrier, inc=1, device_id=pal, device_id_type=MESH)
    expected = jnp.int32(2)
    for s in shifts:
        @pl.when(inside(s))
        def _(s=s):
            pl.semaphore_signal(barrier, inc=1, device_id={"orb": me + s}, device_id_type=MESH)
            far = {"orb": me + s, "fit": pal2["fit"]}
            pl.semaphore_signal(barrier, inc=1, device_id=far, device_id_type=MESH)
        expected = expected + 2 * inside(s).astype(jnp.int32)

    zeros = jnp.zeros((PAD, padded.shape[1]), jnp.float32)
    padded[0:PAD] = zeros
    padded[PAD + dom : 2 * PAD + dom] = zeros

    for table in tables:
        table.wait()
    blocks = owner_ref.shape[0]
    pairs = pair_ref.shape[1]
    wanted = list(range(-reach, reach + 1))

    def find(b, found):
        held = owner_ref[b]
        begin = start_ref[b]
        new = []
        for n, s in enumerate(wanted):
            hit = held == me + s
            new.append((jnp.where(hit, b, found[n][0]), jnp.where(hit, begin, found[n][1])))
        return tuple(new)

    found = tuple((jnp.int32(-1), jnp.int32(0)) for _ in wanted)
    found = lax.fori_loop(0, blocks, find, found, unroll=blocks <= 8)
    my_block, my_start = found[reach]

    def scan(p, listed):
        first = pair_ref[0, p] == my_block
        second = pair_ref[1, p]
        return tuple(
            jnp.where(first & (second == found[slot[s]][0]), 1, listed[n]) for n, s in enumerate(shifts)
        )

    listed = lax.fori_loop(0, pairs, scan, tuple(jnp.int32(0) for _ in shifts), unroll=pairs <= 16)
    listed = dict(zip(shifts, listed))

    pl.semaphore_wait(barrier, expected)

    coeff_out = {}
    for s in [k for k in order if k != 0]:
        coeff_out[s] = remote(
            coeff_hbm.at[low], got.at[slot[-s], low], csend.at[slot[s]], crecv.at[slot[-s]], {"orb": me + s}
        )

        @pl.when(inside(s))
        def _(s=s):
            coeff_out[s].start()

    def arrival(s):
        return remote(
            coeff_hbm.at[low], got.at[slot[s], low], csend.at[slot[-s]], crecv.at[slot[s]], {"orb": me + s}
        )

    def forward(s):
        return remote(got.at[slot[s], low], got.at[slot[s], low], fsend.at[slot[s]], frecv.at[slot[s]], pal1)

    def other_half(s):
        return remote(got.at[slot[s], low], got.at[slot[s], 1 - low], fsend.at[slot[s]], frecv.at[slot[s]], pal1)

    def stage1(s):
        n = slot[s]
        return remote(away.at[n], got1.at[n], send1.at[n], recv1.at[n], pal1)

    def stage2():
        return remote(sum1.at[1 - high], got2, send2, recv2, pal2)

    def stage3(s, across=0):
        return remote(
            coded.at[slot[s], 1 - high if across else high], got3.at[slot[-s], across],
            send3.at[slot[s], across], recv3.at[slot[-s], across],
            {"orb": me + s, "fit": pal2["fit"] if across else fit},
        )

    def encode(value):
        peak = jnp.maximum(jnp.max(jnp.abs(value), axis=0, keepdims=True), 1e-37)
        level = jnp.clip(jnp.ceil(jnp.log2(peak)), -126.0, 127.0)
        part = jnp.floor(level * 0.5)
        steps = value * jnp.exp2(-part) * (jnp.exp2(part - level) * STEPS)
        steps = jnp.clip(jnp.floor(steps + 0.5), -32767.0, 32767.0)
        tail = jnp.broadcast_to(level, (TAIL, value.shape[1]))
        return steps.astype(jnp.int32).astype(jnp.int16), tail.astype(jnp.int32).astype(jnp.int16)

    def decode(ref):
        level = ref[quarter : quarter + TAIL].astype(jnp.int32).astype(jnp.float32)[0:1]
        part = jnp.floor(level * 0.5)
        steps = ref[0:quarter].astype(jnp.int32).astype(jnp.float32)
        return steps * (jnp.exp2(level - part) * (1.0 / STEPS)) * jnp.exp2(part)

    def compute(s):
        a, b = spans[s]
        width = b - a
        if s == 0:
            block = coeff[...]
            offset = jnp.int32(half - a)
        else:
            block = got[slot[s]]
            offset = jnp.clip(
                found[slot[s]][1] - my_start + half - a, max(0, width - dom - PAD), min(PAD, width - dom)
            )
        padded[PAD : PAD + dom] = block.reshape(dom, block.shape[-1]).astype(jnp.float32)
        shifted = padded[pl.ds(PAD - offset, width), :].astype(jnp.bfloat16)
        window = ints[:, a:b]
        fitted = lax.dot_general(
            shifted, window, (((0,), (1,)), ((), ())), preferred_element_type=jnp.float32
        ).astype(jnp.bfloat16)
        wide[0:width] = jnp.dot(fitted, window, preferred_element_type=jnp.float32).T
        for x in range(2):
            away[slot[s], x] = wide[pl.ds(offset + (2 * x + 1 - low) * quarter, quarter), :]
            keep[slot[s], x] = wide[pl.ds(offset + (2 * x + low) * quarter, quarter), :]

    def when(s, do):
        if s == 0:
            do()
        else:
            pl.when(inside(s))(do)

    def pass_on(s):
        def do():
            arrival(s).wait_recv()
            forward(s).start()
        when(s, do)

    def work(s):
        def do():
            if s != 0:
                other_half(s).wait_recv()
            compute(s)
            stage1(s).start()
        when(s, do)

    def first(s):
        def do():
            stage1(s).wait_recv()
            if s == 0:
                sum1[...] = keep[slot[s]] + got1[slot[s]]
                stage2().start()
                return
            for across in (1, 0):
                x = 1 - high if across else high
                total = keep[slot[s], x] + got1[slot[s], x]
                total = jnp.where(listed[s] > 0, total, 0.0)
                coded[slot[s], x, 0:quarter], coded[slot[s], x, quarter : quarter + TAIL] = encode(total)
                stage3(s, across).start()
        when(s, do)

    coeff_copy.wait()
    copies[0].wait()
    work(0)
    for s in order[1:3]:
        pass_on(s)
    first(0)
    for copy in copies[1:]:
        copy.wait()
    for n, s in enumerate(order[1:]):
        work(s)
        if n + 3 < len(order):
            pass_on(order[n + 3])
        if n > 0:
            first(order[n])
    first(order[-1])
    stage2().wait_recv()
    out_ref[...] = sum1[high] + got2[...]
    for s in order[1:]:
        def take(s=s):
            for across in (0, 1):
                stage3(-s, across).wait_recv()
                out_ref[...] += decode(got3.at[slot[s], across])
        when(s, take)

    for s in order:
        def drain(s=s):
            stage1(s).wait_send()
            if s == 0:
                stage2().wait_send()
            else:
                coeff_out[s].wait_send()
                forward(s).wait_send()
                stage3(s).wait_send()
                stage3(s, 1).wait_send()
        when(s, drain)


def local(sizes, half_ints, orbital_coeffs, block_owner, dom_start, pair_list):
    orb_count, fit_count, reach = sizes
    _, fits, occ, win = half_ints.shape
    dom = orbital_coeffs.shape[1]
    ints = half_ints.reshape(fits * occ, win)
    coeffs = orbital_coeffs.reshape(2, dom // 2, occ)
    quarter = dom // fit_count
    slots = 2 * reach + 1
    f32 = jnp.float32
    dma = pltpu.SemaphoreType.DMA
    out = pl.pallas_call(
        functools.partial(kernel, sizes),
        out_shape=jax.ShapeDtypeStruct((quarter, occ), f32),
        in_specs=[pl.BlockSpec(memory_space=pltpu.HBM)] * 5,
        out_specs=pl.BlockSpec(memory_space=pltpu.VMEM),
        scratch_shapes=[
            pltpu.SMEM(block_owner.shape, jnp.int32),
            pltpu.SMEM(dom_start.shape, jnp.int32),
            pltpu.SMEM(pair_list.shape[::-1], jnp.int32),
            dma((3,)),
            pltpu.VMEM((fits * occ, win), jnp.bfloat16),
            pltpu.VMEM((2, dom // 2, occ), jnp.bfloat16),
            pltpu.VMEM((slots, 2, dom // 2, occ), jnp.bfloat16),
            pltpu.VMEM((2 * PAD + dom, occ), f32),
            pltpu.VMEM((dom + 256, occ), f32),
            pltpu.VMEM((slots, 2, quarter, occ), f32),
            pltpu.VMEM((slots, 2, quarter, occ), f32),
            pltpu.VMEM((slots, 2, quarter, occ), f32),
            pltpu.VMEM((2, quarter, occ), f32),
            pltpu.VMEM((quarter, occ), f32),
            pltpu.VMEM((slots, 2, quarter + TAIL, occ), jnp.int16),
            pltpu.VMEM((slots, 2, quarter + TAIL, occ), jnp.int16),
            dma((slots,)),
            dma,
        ] + [dma((slots,))] * 6 + [dma, dma] + [dma((slots, 2))] * 2,
        compiler_params=pltpu.CompilerParams(
            collective_id=0, has_side_effects=True, vmem_limit_bytes=64 * 1024 * 1024
        ),
    )(block_owner, dom_start, pair_list.T, ints, coeffs)
    return out[None]


def solution(mesh):
    orb_count = mesh.shape["orb"]
    sizes = (orb_count, mesh.shape["fit"], min(RANGE, orb_count - 1))
    return jax.shard_map(
        functools.partial(local, sizes),
        mesh=mesh,
        in_specs=(
            P(("bead", "orb"), "fit", None, None),
            P(("bead", "orb"), None, None),
            P("bead"),
            P("bead"),
            P("bead", None),
        ),
        out_specs=P(("bead", "orb"), "fit", None),
        check_vma=False,
    )
```

```python
import functools

import jax
import jax.numpy as jnp
from jax import lax
from jax.experimental import pallas as pl
from jax.experimental.pallas import tpu as pltpu
from jax.sharding import PartitionSpec as P

MESH = pl.DeviceIdType.MESH
STEPS = 16384.0
TAIL = 16
RANGE = 2
SPACING = 448
JIT = 64
LANE = 128
PAD = 192


def columns_of(shift, half, dom, win):
    low = (half + SPACING * shift - JIT + 1) // LANE * LANE
    high = -(-(half + SPACING * shift + JIT - 1 + dom) // LANE) * LANE
    if shift == 0:
        low, high = half // LANE * LANE, -(-(half + dom) // LANE) * LANE
    return max(low, 0), min(high, win)


def kernel(
    sizes, owner_hbm, start_hbm, pair_hbm, ints_hbm, coeff_hbm, out_ref,
    owner_ref, start_ref, pair_ref, table_sem,
    ints, coeff, got, padded, wide, away, keep, got1, sum1, got2, coded, got3,
    ints_sem, coeff_sem, csend, crecv, fsend, frecv, send1, recv1, send2, recv2, send3, recv3,
):
    orb_count, fit_count, reach = sizes
    shifts = [s for s in range(-reach, reach + 1) if s != 0]
    order = [0] + [sign * k for k in range(reach, 0, -1) for sign in (-1, 1)]
    slot = {s: s + reach for s in range(-reach, reach + 1)}
    rows, win = ints.shape
    dom = 2 * coeff.shape[1]
    half = (win - dom) // 2
    quarter = out_ref.shape[0]
    me = lax.axis_index("orb")
    fit = lax.axis_index("fit")
    low = lax.rem(fit, 2)
    high = fit // 2
    pal1 = {"fit": high * 2 + 1 - low}
    pal2 = {"fit": (1 - high) * 2 + low}

    def inside(s):
        return (me + s >= 0) & (me + s < orb_count)

    def remote(src, dst, send, recv, device):
        return pltpu.make_async_remote_copy(
            src_ref=src, dst_ref=dst, send_sem=send, recv_sem=recv,
            device_id=device, device_id_type=MESH,
        )

    barrier = pltpu.get_barrier_semaphore()
    for pal in (pal1, pal2):
        pl.semaphore_signal(barrier, inc=1, device_id=pal, device_id_type=MESH)
    expected = jnp.int32(2)
    for s in shifts:
        @pl.when(inside(s))
        def _(s=s):
            pl.semaphore_signal(barrier, inc=1, device_id={"orb": me + s}, device_id_type=MESH)
            far = {"orb": me + s, "fit": pal2["fit"]}
            pl.semaphore_signal(barrier, inc=1, device_id=far, device_id_type=MESH)
        expected = expected + 2 * inside(s).astype(jnp.int32)

    tables = [
        pltpu.make_async_copy(src, dst, table_sem.at[n])
        for n, (src, dst) in enumerate(
            ((owner_hbm, owner_ref), (start_hbm, start_ref), (pair_hbm, pair_ref))
        )
    ]
    for table in tables:
        table.start()
    coeff_copy = pltpu.make_async_copy(coeff_hbm, coeff, coeff_sem)
    coeff_copy.start()
    spans = {s: columns_of(s, half, dom, win) for s in order}
    cuts = [spans[0]]
    for k in range(1, reach + 1):
        cuts = cuts + [(spans[-k][0], min(c[0] for c in cuts)), (max(c[1] for c in cuts), spans[k][1])]
    copies = []
    for n, (a, b) in enumerate(cuts):
        copy = pltpu.make_async_copy(ints_hbm.at[:, a:b], ints.at[:, a:b], ints_sem.at[n])
        copy.start()
        copies.append(copy)

    pl.semaphore_wait(barrier, expected)

    coeff_out = {}
    for s in [k for k in order if k != 0]:
        coeff_out[s] = remote(
            coeff_hbm.at[low], got.at[slot[-s], low], csend.at[slot[s]], crecv.at[slot[-s]], {"orb": me + s}
        )

        @pl.when(inside(s))
        def _(s=s):
            coeff_out[s].start()

    zeros = jnp.zeros((PAD, padded.shape[1]), jnp.float32)
    padded[0:PAD] = zeros
    padded[PAD + dom : 2 * PAD + dom] = zeros

    for table in tables:
        table.wait()
    blocks = owner_ref.shape[0]
    pairs = pair_ref.shape[1]
    wanted = list(range(-reach, reach + 1))

    def find(b, found):
        held = owner_ref[b]
        begin = start_ref[b]
        new = []
        for n, s in enumerate(wanted):
            hit = held == me + s
            new.append((jnp.where(hit, b, found[n][0]), jnp.where(hit, begin, found[n][1])))
        return tuple(new)

    found = tuple((jnp.int32(-1), jnp.int32(0)) for _ in wanted)
    found = lax.fori_loop(0, blocks, find, found, unroll=blocks <= 8)
    my_block, my_start = found[reach]

    def scan(p, listed):
        first = pair_ref[0, p] == my_block
        second = pair_ref[1, p]
        return tuple(
            jnp.where(first & (second == found[slot[s]][0]), 1, listed[n]) for n, s in enumerate(shifts)
        )

    listed = lax.fori_loop(0, pairs, scan, tuple(jnp.int32(0) for _ in shifts), unroll=pairs <= 16)
    listed = dict(zip(shifts, listed))

    def arrival(s):
        return remote(
            coeff_hbm.at[low], got.at[slot[s], low], csend.at[slot[-s]], crecv.at[slot[s]], {"orb": me + s}
        )

    def forward(s):
        return remote(got.at[slot[s], low], got.at[slot[s], low], fsend.at[slot[s]], frecv.at[slot[s]], pal1)

    def other_half(s):
        return remote(got.at[slot[s], low], got.at[slot[s], 1 - low], fsend.at[slot[s]], frecv.at[slot[s]], pal1)

    def stage1(s):
        n = slot[s]
        return remote(away.at[n], got1.at[n], send1.at[n], recv1.at[n], pal1)

    def stage2():
        return remote(sum1.at[1 - high], got2, send2, recv2, pal2)

    def stage3(s, across=0):
        return remote(
            coded.at[slot[s], 1 - high if across else high], got3.at[slot[-s], across],
            send3.at[slot[s], across], recv3.at[slot[-s], across],
            {"orb": me + s, "fit": pal2["fit"] if across else fit},
        )

    def encode(value):
        peak = jnp.maximum(jnp.max(jnp.abs(value), axis=0, keepdims=True), 1e-37)
        level = jnp.clip(jnp.ceil(jnp.log2(peak)), -126.0, 127.0)
        part = jnp.floor(level * 0.5)
        steps = value * jnp.exp2(-part) * (jnp.exp2(part - level) * STEPS)
        steps = jnp.clip(jnp.floor(steps + 0.5), -32767.0, 32767.0)
        tail = jnp.broadcast_to(level, (TAIL, value.shape[1]))
        return steps.astype(jnp.int32).astype(jnp.int16), tail.astype(jnp.int32).astype(jnp.int16)

    def decode(ref):
        level = ref[quarter : quarter + TAIL].astype(jnp.int32).astype(jnp.float32)[0:1]
        part = jnp.floor(level * 0.5)
        steps = ref[0:quarter].astype(jnp.int32).astype(jnp.float32)
        return steps * jnp.exp2(level - part) * jnp.exp2(part)

    def compute(s):
        a, b = spans[s]
        width = b - a
        if s == 0:
            block = coeff[...]
            offset = jnp.int32(half - a)
        else:
            block = got[slot[s]]
            offset = jnp.clip(
                found[slot[s]][1] - my_start + half - a, max(0, width - dom - PAD), min(PAD, width - dom)
            )
        padded[PAD : PAD + dom] = block.reshape(dom, block.shape[-1]).astype(jnp.float32)
        shifted = padded[pl.ds(PAD - offset, width), :].astype(jnp.bfloat16)
        window = ints[:, a:b]
        fitted = lax.dot_general(
            shifted, window, (((0,), (1,)), ((), ())), preferred_element_type=jnp.float32
        ).astype(jnp.bfloat16)
        wide[0:width] = jnp.dot(fitted, window, preferred_element_type=jnp.float32).T
        for x in range(2):
            away[slot[s], x] = wide[pl.ds(offset + (2 * x + 1 - low) * quarter, quarter), :]
            keep[slot[s], x] = wide[pl.ds(offset + (2 * x + low) * quarter, quarter), :]

    def when(s, do):
        if s == 0:
            do()
        else:
            pl.when(inside(s))(do)

    def pass_on(s):
        def do():
            arrival(s).wait_recv()
            forward(s).start()
        when(s, do)

    def work(s):
        def do():
            if s != 0:
                other_half(s).wait_recv()
            compute(s)
            stage1(s).start()
        when(s, do)

    def first(s):
        def do():
            stage1(s).wait_recv()
            if s == 0:
                sum1[...] = keep[slot[s]] + got1[slot[s]]
                stage2().start()
                return
            for across in (1, 0):
                x = 1 - high if across else high
                total = keep[slot[s], x] + got1[slot[s], x]
                total = jnp.where(listed[s] > 0, total, 0.0)
                coded[slot[s], x, 0:quarter], coded[slot[s], x, quarter : quarter + TAIL] = encode(total)
                stage3(s, across).start()
        when(s, do)

    coeff_copy.wait()
    copies[0].wait()
    work(0)
    for s in order[1:3]:
        pass_on(s)
    first(0)
    for copy in copies[1:]:
        copy.wait()
    for n, s in enumerate(order[1:]):
        work(s)
        if n + 3 < len(order):
            pass_on(order[n + 3])
        if n > 0:
            first(order[n])
    first(order[-1])
    stage2().wait_recv()
    out_ref[...] = (sum1[high] + got2[...]) * STEPS
    for s in order[1:]:
        def take(s=s):
            for across in (0, 1):
                stage3(-s, across).wait_recv()
                out_ref[...] += decode(got3.at[slot[s], across])
        when(s, take)

    for s in order:
        def drain(s=s):
            stage1(s).wait_send()
            if s == 0:
                stage2().wait_send()
            else:
                coeff_out[s].wait_send()
                forward(s).wait_send()
                stage3(s).wait_send()
                stage3(s, 1).wait_send()
        when(s, drain)


def local(sizes, half_ints, orbital_coeffs, block_owner, dom_start, pair_list):
    orb_count, fit_count, reach = sizes
    _, fits, occ, win = half_ints.shape
    dom = orbital_coeffs.shape[1]
    ints = half_ints.reshape(fits * occ, win)
    coeffs = orbital_coeffs.reshape(2, dom // 2, occ)
    quarter = dom // fit_count
    slots = 2 * reach + 1
    f32 = jnp.float32
    dma = pltpu.SemaphoreType.DMA
    out = pl.pallas_call(
        functools.partial(kernel, sizes),
        out_shape=jax.ShapeDtypeStruct((quarter, occ), f32),
        in_specs=[pl.BlockSpec(memory_space=pltpu.HBM)] * 5,
        out_specs=pl.BlockSpec(memory_space=pltpu.VMEM),
        scratch_shapes=[
            pltpu.SMEM(block_owner.shape, jnp.int32),
            pltpu.SMEM(dom_start.shape, jnp.int32),
            pltpu.SMEM(pair_list.shape[::-1], jnp.int32),
            dma((3,)),
            pltpu.VMEM((fits * occ, win), jnp.bfloat16),
            pltpu.VMEM((2, dom // 2, occ), jnp.bfloat16),
            pltpu.VMEM((slots, 2, dom // 2, occ), jnp.bfloat16),
            pltpu.VMEM((2 * PAD + dom, occ), f32),
            pltpu.VMEM((dom + 256, occ), f32),
            pltpu.VMEM((slots, 2, quarter, occ), f32),
            pltpu.VMEM((slots, 2, quarter, occ), f32),
            pltpu.VMEM((slots, 2, quarter, occ), f32),
            pltpu.VMEM((2, quarter, occ), f32),
            pltpu.VMEM((quarter, occ), f32),
            pltpu.VMEM((slots, 2, quarter + TAIL, occ), jnp.int16),
            pltpu.VMEM((slots, 2, quarter + TAIL, occ), jnp.int16),
            dma((slots,)),
            dma,
        ] + [dma((slots,))] * 6 + [dma, dma] + [dma((slots, 2))] * 2,
        compiler_params=pltpu.CompilerParams(
            collective_id=0, has_side_effects=True, vmem_limit_bytes=64 * 1024 * 1024
        ),
    )(block_owner, dom_start, pair_list.T, ints, coeffs)
    return out[None] * (1.0 / STEPS)


def solution(mesh):
    orb_count = mesh.shape["orb"]
    sizes = (orb_count, mesh.shape["fit"], min(RANGE, orb_count - 1))
    return jax.shard_map(
        functools.partial(local, sizes),
        mesh=mesh,
        in_specs=(
            P(("bead", "orb"), "fit", None, None),
            P(("bead", "orb"), None, None),
            P("bead"),
            P("bead"),
            P("bead", None),
        ),
        out_specs=P(("bead", "orb"), "fit", None),
        check_vma=False,
    )
```
